512 devices in a mesh: ctx: 64 (over z_lo, y, core), ch: 8 (over z_hi, x).
Axes of the slice: x: 4, y: 4, z: 16 (z_hi: 2, z_lo: 8; z = z_hi * 8 + z_lo), core: 2. Of those that a mesh axis runs over, the one named last changes fastest.
Arguments:
- queries: bfloat16 [8192, 4096], P('ctx', 'ch'), may hold values from -6 to 6
- keys: bfloat16 [8192, 4096], P('ctx', 'ch'), may hold values from -6 to 6
- values: bfloat16 [8192, 4096], P('ctx', 'ch'), may hold values from -6 to 6
- conv_out: bfloat16 [8192, 4096], P('ctx', 'ch'), may hold values from -6 to 6
- filters: bfloat16 [8192, 4096], P('ctx', 'ch'), may hold values from -1.2 to 1.2
- out_grad: bfloat16 [8192, 4096], P('ctx', 'ch'), may hold values from -16 to 16
- out_weight: bfloat16 [4096, 4096], P('ctx', 'ch'), may hold values from -0.09375 to 0.09375
- moment_one: float32 [4096, 4096], P('ctx', 'ch'), may hold values from -64 to 64
- moment_two: float32 [4096, 4096], P('ctx', 'ch'), may hold values from 200 to 2000
Outputs:
- query_grad: bfloat16 [8192, 4096], P('ctx', 'ch')
- key_grad: bfloat16 [8192, 4096], P('ctx', 'ch')
- value_grad: bfloat16 [8192, 4096], P('ctx', 'ch')
- filter_grad: bfloat16 [8192, 4096], P('ctx', 'ch')
- new_weight: bfloat16 [4096, 4096], P('ctx', 'ch')
- new_moment_one: float32 [4096, 4096], P('ctx', 'ch')
- new_moment_two: float32 [4096, 4096], P('ctx', 'ch')
The draws below stay inside these ranges and needn't reach their ends.
All inputs are finite; a program needn't handle non-finite values.
Results may differ from the reference program's by a relative error of at most 0.0058.
Values may be sent and summed in bfloat16 or wider, within the bound.
A program may use at most 64 MiB of HBM per device.

```python
import math
import jax
import jax.numpy as jnp
from jax import lax

D = 4096
TOKENS = 8192


def draw_filters(key, part):
    key = jax.random.fold_in(key, 11)
    noise_key, length_key, drop_key = jax.random.split(key, 3)
    token_position = jnp.arange(TOKENS, dtype=jnp.int32)[:, None]
    low = jnp.log(jnp.float32(30.0))
    high = jnp.log(jnp.float32(4 * TOKENS))
    falloff_length = jnp.exp(jax.random.uniform(length_key, (1, D), jnp.float32, low, high))
    dropout_flags = jax.random.randint(drop_key, (4, 1, D), 0, TOKENS)
    impulse_spike = jnp.prod(jnp.where(token_position[None] >= dropout_flags, 0.6, 1.0).astype(jnp.float32), axis=0)
    decay_envelope = jnp.exp(-token_position.astype(jnp.float32) / falloff_length) * impulse_spike
    decay_envelope = decay_envelope * jnp.sqrt(2.0 / jnp.minimum(falloff_length, jnp.float32(TOKENS)))
    noise = jax.random.truncated_normal(noise_key, -4.0, 4.0, (TOKENS, D), jnp.float32)
    return (noise * decay_envelope).astype(jnp.bfloat16)


def raised(result, stream_key, source, target, parts, factor):
    owner, partner = [(jnp.arange(result.shape[position]) // (result.shape[position] // parts)).reshape([-1 if axis == position else 1 for axis in range(result.ndim)]) for position in (source, target)]
    chosen = jax.random.permutation(stream_key, parts)[partner]
    strong = (owner == chosen) | (owner == (partner + parts // 2) % parts)
    return jnp.where(strong, factor * result, result)


def steps_of(key, shape, cuts, low, top_value):
    loudness, own = 1.0, jax.random.fold_in(key, 6)
    for axis_at, parts in cuts:
        steps = jnp.exp(jax.random.uniform(jax.random.fold_in(own, axis_at), (parts,), jnp.float32, low / len(cuts), top_value / len(cuts)))
        loudness = loudness * jnp.repeat(steps, shape[axis_at] // parts).reshape([-1 if axis == axis_at else 1 for axis in range(len(shape))])
    return loudness


def bell_draw(stream_key, shape, spread, most, cuts=(), held_as=jnp.bfloat16):
    drawn = spread * jax.random.normal(stream_key, shape, jnp.float32)
    if cuts:
        drawn = drawn * steps_of(stream_key, shape, cuts, -0.22, 0.18)
    return jnp.clip(drawn, -most, most).astype(held_as)


def bell_draw_with(rng, shape, scale, reach, shards, heavy, held_as=jnp.bfloat16):
    entries = scale * jax.random.normal(rng, shape, jnp.float32)
    if shards:
        entries = entries * steps_of(rng, shape, shards, -0.22, 0.18)
    return jnp.clip(raised(entries, jax.random.fold_in(rng, 3), *heavy), -reach, reach).astype(held_as)


def setup_inputs(seed: int = 0) -> dict:
    streams_of = jax.random.split(jax.random.key(seed), 10)
    return {
        "queries": bell_draw(streams_of[0], (TOKENS, D), 1.0, 6.0, ((0, 64), (1, 8))),
        "keys": bell_draw(streams_of[1], (TOKENS, D), 1.0, 6.0, ((0, 64), (1, 8))),
        "values": bell_draw(streams_of[2], (TOKENS, D), 1.0, 6.0, ((0, 64), (1, 8))),
        "conv_out": bell_draw(streams_of[3], (TOKENS, D), 1.0, 6.0, ((0, 64), (1, 8))),
        "filters": draw_filters(jax.random.fold_in(streams_of[9], 71), 0),
        "out_grad": bell_draw_with(streams_of[5], (TOKENS, D), 1.0, 16.0, ((0, 64), (1, 8)), (0, 1, 64, 4.0)),
        "out_weight": bell_draw(streams_of[6], (D, D), D ** -0.5, 0.09375, ((0, 64), (1, 8))),
        "moment_one": bell_draw(streams_of[7], (D, D), 12.0, 64.0, ((0, 64), (1, 8)), jnp.float32),
        "moment_two": jnp.clip(jnp.exp(math.log(2000.0) - 2.3025851 * jax.random.uniform(streams_of[8], (D, D), jnp.float32) ** steps_of(streams_of[8], (D, D), ((0, 64), (1, 8)), -0.2, 0.2)), 200.0, 2000.0),
    }


BETA_ONE = 0.9
BETA_TWO = 0.95
STEP_RATE = 0.003
DECAY = 0.1
ADAM_STABILIZER = 1e-08

def correlate(items):
    conv_grad, filt, key_value = items
    length = conv_grad.shape[-1]
    spec_grad = jnp.fft.fft(conv_grad.astype(jnp.float32), n=2 * length, axis=-1)
    spec_filt = jnp.fft.fft(filt.astype(jnp.float32), n=2 * length, axis=-1)
    spec_pair = jnp.fft.fft(key_value.astype(jnp.float32), n=2 * length, axis=-1)
    value_delta = jnp.real(jnp.fft.ifft(jnp.conj(spec_filt) * spec_grad, axis=-1))[:, :length]
    filter_grad = jnp.real(jnp.fft.ifft(jnp.conj(spec_pair) * spec_grad, axis=-1))[:, :length]
    return (value_delta.astype(jnp.bfloat16), filter_grad.astype(jnp.bfloat16))

def reference(queries, keys, values, conv_out, filters, out_grad, out_weight, moment_one, moment_two):
    out_delta = jnp.dot(out_grad, out_weight, preferred_element_type=jnp.float32)
    query_float = queries.astype(jnp.float32)
    convolved_single = conv_out.astype(jnp.float32)
    proj_in = (query_float * convolved_single).astype(jnp.bfloat16)
    weight_grad = lax.dot_general(out_grad, proj_in, (((0,), (0,)), ((), ())), preferred_element_type=jnp.float32)
    query_grad = (out_delta * convolved_single).astype(jnp.bfloat16)
    conv_grad = (out_delta * query_float).astype(jnp.bfloat16)
    key_value = (keys.astype(jnp.float32) * values.astype(jnp.float32)).astype(jnp.bfloat16)
    width = min(D, 128)

    def blocks(array):
        return array.T.reshape(D // width, width, TOKENS)
    delta_blocks, filt_blocks = lax.map(correlate, (blocks(conv_grad), blocks(filters), blocks(key_value)))
    value_delta = delta_blocks.reshape(D, TOKENS).T
    filter_grad = filt_blocks.reshape(D, TOKENS).T
    key_grad = (value_delta.astype(jnp.float32) * values.astype(jnp.float32)).astype(jnp.bfloat16)
    value_grad = (value_delta.astype(jnp.float32) * keys.astype(jnp.float32)).astype(jnp.bfloat16)
    new_moment_one = BETA_ONE * moment_one + (1.0 - BETA_ONE) * weight_grad
    new_moment_two = BETA_TWO * moment_two + (1.0 - BETA_TWO) * weight_grad * weight_grad
    corr_one = 1.0 - BETA_ONE ** 10
    corr_two = 1.0 - BETA_TWO ** 10
    weight_float = out_weight.astype(jnp.float32)
    update = new_moment_one / corr_one / (jnp.sqrt(new_moment_two / corr_two) + ADAM_STABILIZER)
    new_weight = (weight_float - STEP_RATE * (update + DECAY * weight_float)).astype(jnp.bfloat16)
    return (query_grad, key_grad, value_grad, filter_grad, new_weight, new_moment_one, new_moment_two)
```

```python
import math

import jax
import jax.numpy as jnp
import numpy as np
from jax import lax
from jax.experimental import pallas as pl
from jax.experimental.pallas import tpu as pltpu
from jax.sharding import PartitionSpec as P

BETA_ONE = 0.9
BETA_TWO = 0.95
STEP_RATE = 0.003
DECAY = 0.1
ADAM_STABILIZER = 1e-08

MESH = pl.DeviceIdType.MESH
F32 = jnp.float32
BF16 = jnp.bfloat16
HALF = 72


def halves(table):
    high = table.astype(np.float32).astype(BF16)
    low = (table.astype(np.float32) - high.astype(np.float32)).astype(BF16)
    return high, low


def dft_tables():
    k = np.arange(HALF)[:, None]
    j = np.arange(64)[None, :]
    outer = 2.0 * math.pi * ((k * j) % 128) / 128
    first = np.concatenate([np.cos(outer), -np.sin(outer)], axis=0)
    first = np.concatenate(halves(first), axis=0)
    swapped = np.concatenate([first[:, 0::2], first[:, 1::2]], axis=1)
    m = np.arange(128)[None, :]
    turn = 2.0 * math.pi * (k * m) / 16384
    twist = np.stack([np.cos(turn), np.sin(turn)]).astype(np.float32)
    inner = 2.0 * math.pi * ((np.arange(128)[:, None] * m) % 128) / 128
    c, s = np.cos(inner), np.sin(inner)
    forth = np.stack(halves(np.block([[c, -s], [s, c]])))
    back = np.stack(halves(np.block([[c, s], [-s, c]])))
    weight = np.where((k == 0) | (k == 64), 1.0, np.where(k < 64, 2.0, 0.0)) / 16384
    last = np.concatenate([weight * np.cos(outer), -weight * np.sin(outer)], axis=0).T
    last = np.stack(halves(last))
    return first, swapped, twist, forth, back, last


def three(left, high, low):
    left_high = left.astype(BF16)
    left_low = (left - left_high.astype(F32)).astype(BF16)
    return (
        jnp.dot(left_high, high, preferred_element_type=F32)
        + jnp.dot(left_low, high, preferred_element_type=F32)
        + jnp.dot(left_high, low, preferred_element_type=F32)
    )


def kernel(
    q_ref, k_ref, v_ref, z_ref, h_ref, g_ref, w_ref,
    first_ref, swapped_ref, twist_ref, forth_ref, back_ref, last_ref,
    qg_ref, vd_ref, fg_ref, wg_ref,
    ga, gp, wa, pa, skf, rkf, s1, r1, acc1, sc, rc, acc2, sa, ra, sb, rb, sd, rd,
    sg, rg, sf, rf, fs, dd, aa, spec, xx,
    grad_s, grad_r, gp_s, gp_r, w_s, w_r, p_s, p_r, kf_s, kf_r, one_s, one_r, two_s, two_r,
    g_s, g_r, f_s, f_r,
):
    ctx, ch = lax.axis_index("ctx"), lax.axis_index("ch")
    zl, y, core = ctx // 8, (ctx // 2) % 4, ctx % 2
    chip = ctx // 2
    x, zh = ch % 4, ch // 4
    sib = (chip * 2 + 1 - core, ch)
    far = (ctx, lax.rem(ch + 4, 8))
    z1 = zl + 1 - 2 * (zl % 2)
    z2 = zl + 2 - 4 * ((zl // 2) % 2)
    z4 = lax.rem(zl + 4, 8)

    def place(zz):
        return (zz * 8 + y * 2 + core, ch)

    def remote(src, dst, send, recv, device):
        return pltpu.make_async_remote_copy(
            src_ref=src, dst_ref=dst, send_sem=send, recv_sem=recv, device_id=device, device_id_type=MESH
        )

    def drain(ref, sem):
        pltpu.make_async_copy(ref, ref, sem).wait()

    entry = pltpu.get_barrier_semaphore()

    def greet(d, carry):
        pl.semaphore_signal(entry, 1, device_id=(lax.rem(ctx + d, 64), ch), device_id_type=MESH)
        return carry

    lax.fori_loop(1, 64, greet, 0)

    def near(d):
        x_to, y_to = lax.rem(x + d // 4, 4), lax.rem(y + d % 4, 4)
        return x_to, y_to, (zl * 8 + y_to * 2 + core, zh * 4 + x_to)

    def greet_near(d, carry):
        pl.semaphore_signal(entry, 1, device_id=near(d)[2], device_id_type=MESH)
        return carry

    lax.fori_loop(4, 16, greet_near, 0)
    pl.semaphore_signal(entry, 1, device_id=far, device_id_type=MESH)

    pa[y] = (q_ref[...].astype(F32) * z_ref[...].astype(F32)).astype(BF16)
    wa[zl, core] = w_ref[...]

    def stage_pair(t, carry):
        cols = pl.ds(pl.multiple_of(t * 128, 128), 128)
        kv = (k_ref[:, cols].astype(F32) * v_ref[:, cols].astype(F32)).T.reshape(16, 8, 128)
        filt = h_ref[:, cols].astype(F32).T.reshape(16, 8, 128)
        skf[pl.ds(t * 16, 16)] = jnp.concatenate([kv, filt], axis=1).astype(BF16)
        return carry

    lax.fori_loop(0, 4, stage_pair, 0)
    rkf[ctx] = skf[ctx]
    pl.semaphore_wait(entry, 76)

    far_copy = remote(g_ref, gp, gp_s, gp_r, far)
    far_copy.start()

    def send_w(block, device, step):
        return remote(wa.at[block, core], wa.at[block, core], w_s.at[step], w_r.at[step], device)

    send_w(zl, place(z4), 0).start()
    send_w(zl, sib, 3).start()

    def spread(src, row, half):
        def body(d, carry):
            x_to, y_to, device = near(d)
            cols = pl.ds(pl.multiple_of(y_to * 128, 128), 128)
            remote(src.at[:, cols], ga.at[row, x * 4 + y], grad_s.at[half], grad_r.at[half], device).start()
            return carry

        lax.fori_loop(1, 16, body, 0)
        ga[row, x * 4 + y] = src[:, pl.ds(pl.multiple_of(y * 128, 128), 128)]

    spread(g_ref, zh, 0)
    for d in range(1, 4):
        y_to = lax.rem(y + d, 4)
        remote(pa.at[y], pa.at[y], p_s, p_r, (zl * 8 + y_to * 2 + core, ch)).start()

    drain(wa.at[0, 0], w_r.at[0])
    send_w(zl, place(z2), 1).start()
    send_w(z4, place(z2), 1).start()
    send_w(z4, sib, 3).start()
    drain(wa.at[pl.ds(0, 2), 0], w_r.at[1])
    z24 = lax.rem(z2 + 4, 8)
    for block in (zl, z4, z2, z24):
        send_w(block, place(z1), 2).start()
    send_w(z2, sib, 3).start()
    send_w(z24, sib, 3).start()

    far_copy.wait_recv()
    spread(gp, 1 - zh, 1)

    def send_pair(d, carry):
        to = lax.rem(ctx + d, 64)
        remote(skf.at[to], rkf.at[ctx], kf_s, kf_r, (to, ch)).start()
        return carry

    lax.fori_loop(1, 64, send_pair, 0)

    drain(wa.at[pl.ds(0, 4), 0], w_r.at[2])
    for block in (z1, lax.rem(z1 + 4, 8), z1 + 2 - 4 * ((z1 // 2) % 2), lax.rem(z1 + 6 - 4 * ((z1 // 2) % 2), 8)):
        send_w(block, sib, 3).start()
    drain(wa.at[:, 0], w_r.at[3])
    drain(ga.at[0, pl.ds(0, 15)], grad_r.at[0])

    acc1[...] = jnp.zeros_like(acc1)

    def multiply(row):
        def body(t, carry):
            left = ga[row, pl.ds(t * 4, 4)].reshape(512, 128)
            right = wa[row * 4 + t].reshape(128, 512)
            acc1[...] += jnp.dot(left, right, preferred_element_type=F32)
            return carry

        lax.fori_loop(0, 4, body, 0)

    multiply(zh)
    drain(ga.at[0, pl.ds(0, 15)], grad_r.at[1])
    multiply(1 - zh)
    for d in range(1, 4):
        y_to = lax.rem(y + d, 4)
        s1[d - 1] = acc1[pl.ds(pl.multiple_of(y_to * 128, 128), 128), :].astype(BF16)
        remote(s1.at[d - 1], r1.at[d - 1], one_s, one_r, (zl * 8 + y_to * 2 + core, ch)).start()

    drain(pa.at[pl.ds(0, 3)], p_r)
    first_core = core == 0

    def partial_rows(t, carry):
        left = ga[t // 4, pl.ds((t % 4) * 4, 4)].reshape(512, 128)
        part = lax.dot_general(
            left, pa[...].reshape(512, 512), (((0,), (0,)), ((), ())), preferred_element_type=F32
        )
        top, low = part[:64], part[64:]
        acc2[t] = jnp.where(first_core, top, low)
        sc[t] = jnp.where(first_core, low, top).astype(BF16)
        return carry

    lax.fori_loop(0, 8, partial_rows, 0)
    core_copy = remote(sc, rc, two_s.at[0], two_r.at[0], sib)
    core_copy.start()

    drain(r1, one_r)
    delta = acc1[pl.ds(pl.multiple_of(y * 128, 128), 128), :]
    for d in range(3):
        delta = delta + r1[d].astype(F32)
    qg_ref[...] = (delta * z_ref[...].astype(F32)).astype(BF16)
    conv = (delta * q_ref[...].astype(F32)).astype(BF16).astype(F32)
    sg[...] = conv.T.reshape(32, 16, 128).astype(BF16)
    rg[core, chip] = sg[chip]

    def send_conv(d, carry):
        to = lax.rem(chip + d, 32)
        remote(sg.at[to], rg.at[core, chip], g_s.at[0], g_r.at[0], (to * 2 + core, ch)).start()
        return carry

    lax.fori_loop(1, 32, send_conv, 0)

    core_copy.wait_recv()
    bit0, bit1, bit2 = zl % 2, (zl // 2) % 2, zl // 4
    for i in range(4):
        give, keep = 2 * i + 1 - bit0, 2 * i + bit0
        sa[i] = (acc2[give] + rc[give].astype(F32)).astype(BF16)
        acc2[keep] = acc2[keep] + rc[keep].astype(F32)
    a_copy = remote(sa, ra, two_s.at[1], two_r.at[1], place(z1))
    a_copy.start()

    twist_cos, twist_sin = twist_ref[0], twist_ref[1]

    def spectrum(base, table, slot):
        for c in range(8):
            dd[:, c * 128 : (c + 1) * 128] = fs[pl.ds(base + c, 64, stride=16), :].astype(BF16)
        both = jnp.dot(table[...], dd[...], preferred_element_type=F32)
        both = both[: 2 * HALF] + both[2 * HALF :]
        for c in range(8):
            real = both[:HALF, c * 128 : (c + 1) * 128]
            imag = both[HALF:, c * 128 : (c + 1) * 128]
            aa[c * HALF : (c + 1) * HALF, :128] = real * twist_cos + imag * twist_sin
            aa[c * HALF : (c + 1) * HALF, 128:] = imag * twist_cos - real * twist_sin
        spec[slot] = three(aa[...], forth_ref[0], forth_ref[1])

    drain(rkf.at[pl.ds(0, 63)], kf_r)
    fs[...] = rkf[...].astype(F32).reshape(1024, 128)
    spectrum(0, first_ref, 0)
    spectrum(8, first_ref, 1)

    a_copy.wait_recv()
    for i in range(2):
        give, keep = 2 * i + 1 - bit1, 2 * i + bit1
        sb[i] = (acc2[2 * give + bit0] + ra[give].astype(F32)).astype(BF16)
        acc2[2 * keep + bit0] = acc2[2 * keep + bit0] + ra[keep].astype(F32)
    b_copy = remote(sb, rb, two_s.at[2], two_r.at[2], place(z2))
    b_copy.start()

    drain(rg.at[0, pl.ds(0, 31)], g_r.at[0])
    g_copy = remote(rg.at[core], rg.at[core], g_s.at[1], g_r.at[1], sib)
    g_copy.start()

    b_copy.wait_recv()
    give, keep = 1 - bit2, bit2
    sd[...] = (acc2[4 * give + 2 * bit1 + bit0] + rb[give].astype(F32)).astype(BF16)
    d_copy = remote(sd, rd, two_s.at[3], two_r.at[3], place(z4))
    d_copy.start()
    mine = acc2[4 * keep + 2 * bit1 + bit0] + rb[keep].astype(F32)
    wg_ref[...] = mine

    g_copy.wait_recv()
    fs[...] = rg[...].astype(F32).reshape(1024, 128)
    spectrum(core * 8, swapped_ref, 2)

    for slot, base in ((1, 0), (0, 8)):
        other_real, other_imag = spec[slot, :, :128], spec[slot, :, 128:]
        grad_real, grad_imag = spec[2, :, :128], spec[2, :, 128:]
        aa[:, :128] = other_real * grad_real + other_imag * grad_imag
        aa[:, 128:] = other_real * grad_imag - other_imag * grad_real
        turned = three(aa[...], back_ref[0], back_ref[1])
        for c in range(8):
            real = turned[c * HALF : (c + 1) * HALF, :128]
            imag = turned[c * HALF : (c + 1) * HALF, 128:]
            xx[:HALF, c * 128 : (c + 1) * 128] = real * twist_cos - imag * twist_sin
            xx[HALF:, c * 128 : (c + 1) * 128] = real * twist_sin + imag * twist_cos
        right = xx[...]
        right_high = right.astype(BF16)
        right_low = (right - right_high.astype(F32)).astype(BF16)
        signal = (
            jnp.dot(last_ref[0], right_high, preferred_element_type=F32)
            + jnp.dot(last_ref[0], right_low, preferred_element_type=F32)
            + jnp.dot(last_ref[1], right_high, preferred_element_type=F32)
        )
        for c in range(8):
            fs[pl.ds(base + c, 64, stride=16), :] = signal[:, c * 128 : (c + 1) * 128]
    sf[...] = fs[...].astype(BF16).reshape(64, 16, 128)
    rf[ctx] = sf[ctx]

    def send_back(d, carry):
        to = lax.rem(ctx + d, 64)
        remote(sf.at[to], rf.at[ctx], f_s, f_r, (to, ch)).start()
        return carry

    lax.fori_loop(1, 64, send_back, 0)

    d_copy.wait_recv()
    wg_ref[...] = wg_ref[...] + rd[...].astype(F32)

    far_copy.wait_send()
    drain(wa.at[0, 0], w_s.at[0])
    drain(wa.at[pl.ds(0, 2), 0], w_s.at[1])
    drain(wa.at[pl.ds(0, 4), 0], w_s.at[2])
    drain(wa.at[:, 0], w_s.at[3])
    drain(ga.at[0, pl.ds(0, 15)], grad_s.at[0])
    drain(ga.at[0, pl.ds(0, 15)], grad_s.at[1])
    drain(pa.at[pl.ds(0, 3)], p_s)
    drain(skf.at[pl.ds(0, 63)], kf_s)
    drain(s1, one_s)
    core_copy.wait_send()
    a_copy.wait_send()
    b_copy.wait_send()
    d_copy.wait_send()
    drain(sg.at[pl.ds(0, 31)], g_s.at[0])
    g_copy.wait_send()

    drain(rf.at[pl.ds(0, 63)], f_r)
    for t in range(4):
        back = rf[t * 16 : (t + 1) * 16].astype(F32)
        vd_ref[:, t * 128 : (t + 1) * 128] = back[:, :8].reshape(128, 128).T.astype(BF16)
        fg_ref[:, t * 128 : (t + 1) * 128] = back[:, 8:].reshape(128, 128).T.astype(BF16)
    drain(sf.at[pl.ds(0, 63)], f_s)


def on_device(
    queries, keys, values, conv_out, filters, out_grad, out_weight, moment_one, moment_two
):
    tables = [jnp.asarray(t) for t in dft_tables()]
    vmem = pl.BlockSpec(memory_space=pltpu.VMEM)
    dma = pltpu.SemaphoreType.DMA

    def half(*shape):
        return pltpu.VMEM(shape, BF16)

    def full(*shape):
        return pltpu.VMEM(shape, F32)

    query_grad, value_delta, filter_grad, weight_grad = pl.pallas_call(
        kernel,
        out_shape=(
            jax.ShapeDtypeStruct((128, 512), BF16),
            jax.ShapeDtypeStruct((128, 512), BF16),
            jax.ShapeDtypeStruct((128, 512), BF16),
            jax.ShapeDtypeStruct((64, 512), F32),
        ),
        in_specs=[vmem] * 13,
        out_specs=(vmem,) * 4,
        scratch_shapes=[
            half(2, 16, 128, 128),
            half(128, 512),
            half(8, 2, 64, 512),
            half(4, 128, 512),
            half(64, 16, 128),
            half(64, 16, 128),
            half(3, 128, 512),
            half(3, 128, 512),
            full(512, 512),
            half(8, 64, 512),
            half(8, 64, 512),
            full(8, 64, 512),
            half(4, 64, 512),
            half(4, 64, 512),
            half(2, 64, 512),
            half(2, 64, 512),
            half(64, 512),
            half(64, 512),
            half(32, 16, 128),
            half(2, 32, 16, 128),
            half(64, 16, 128),
            half(64, 16, 128),
            full(1024, 128),
            half(64, 1024),
            full(8 * HALF, 256),
            full(3, 8 * HALF, 256),
            full(2 * HALF, 1024),
            dma((2,)), dma((2,)),
            dma, dma,
            dma((4,)), dma((4,)),
            dma, dma,
            dma, dma,
            dma, dma,
            dma((4,)), dma((4,)),
            dma((2,)), dma((2,)),
            dma, dma,
        ],
        compiler_params=pltpu.CompilerParams(
            collective_id=1, has_side_effects=True, vmem_limit_bytes=40 * 2**20
        ),
    )(queries, keys, values, conv_out, filters, out_grad, out_weight, *tables)

    delta = value_delta.astype(F32)
    key_grad = (delta * values.astype(F32)).astype(BF16)
    value_grad = (delta * keys.astype(F32)).astype(BF16)
    new_moment_one = BETA_ONE * moment_one + (1.0 - BETA_ONE) * weight_grad
    new_moment_two = BETA_TWO * moment_two + (1.0 - BETA_TWO) * weight_grad * weight_grad
    corr_one = 1.0 - BETA_ONE**10
    corr_two = 1.0 - BETA_TWO**10
    weight_float = out_weight.astype(F32)
    update = new_moment_one / corr_one / (jnp.sqrt(new_moment_two / corr_two) + ADAM_STABILIZER)
    new_weight = (weight_float - STEP_RATE * (update + DECAY * weight_float)).astype(BF16)
    return (
        query_grad,
        key_grad,
        value_grad,
        filter_grad,
        new_weight,
        new_moment_one,
        new_moment_two,
    )


def solution(mesh):
    spec = P("ctx", "ch")
    return jax.shard_map(
        on_device, mesh=mesh, in_specs=(spec,) * 9, out_specs=(spec,) * 7, check_vma=False
    )
```

```python
import math

import jax
import jax.numpy as jnp
import numpy as np
from jax import lax
from jax.experimental import pallas as pl
from jax.experimental.pallas import tpu as pltpu
from jax.sharding import PartitionSpec as P

BETA_ONE = 0.9
BETA_TWO = 0.95
STEP_RATE = 0.003
DECAY = 0.1
ADAM_STABILIZER = 1e-08

MESH = pl.DeviceIdType.MESH
F32 = jnp.float32
BF16 = jnp.bfloat16
HALF = 72


def halves(table):
    high = table.astype(np.float32).astype(BF16)
    low = (table.astype(np.float32) - high.astype(np.float32)).astype(BF16)
    return high, low


def dft_tables():
    k = np.arange(HALF)[:, None]
    j = np.arange(64)[None, :]
    outer = 2.0 * math.pi * ((k * j) % 128) / 128
    first = np.concatenate([np.cos(outer), -np.sin(outer)], axis=0)
    first = np.concatenate(halves(first), axis=0)
    swapped = np.concatenate([first[:, 0::2], first[:, 1::2]], axis=1)
    m = np.arange(128)[None, :]
    turn = 2.0 * math.pi * (k * m) / 16384
    twist = np.stack([np.cos(turn), np.sin(turn)]).astype(np.float32)
    inner = 2.0 * math.pi * ((np.arange(128)[:, None] * m) % 128) / 128
    c, s = np.cos(inner), np.sin(inner)
    forth = np.stack(halves(np.block([[c, -s], [s, c]])))
    back = np.stack(halves(np.block([[c, s], [-s, c]])))
    weight = np.where((k == 0) | (k == 64), 1.0, np.where(k < 64, 2.0, 0.0)) / 16384
    last = np.concatenate([weight * np.cos(outer), -weight * np.sin(outer)], axis=0).T
    last = np.stack(halves(last))
    return first, swapped, twist, forth, back, last


def three(left, high, low):
    left_high = left.astype(BF16)
    left_low = (left - left_high.astype(F32)).astype(BF16)
    return (
        jnp.dot(left_high, high, preferred_element_type=F32)
        + jnp.dot(left_low, high, preferred_element_type=F32)
        + jnp.dot(left_high, low, preferred_element_type=F32)
    )


def kernel(
    q_in, k_in, v_in, z_in, h_in, g_in, w_in,
    first_in, swapped_in, twist_in, forth_in, back_in, last_in,
    qg_ref, vd_ref, fg_ref, wg_ref,
    q_ref, k_ref, v_ref, z_ref, h_ref, g_ref,
    first_ref, swapped_ref, twist_ref, forth_ref, back_ref, last_ref,
    ga, gp, wa, pa, skf, rkf, s1, r1, acc1, sc, rc, acc2, sa, ra, sb, rb, sd, rd,
    sg, rg, sf, rf, fs, dd, aa, spec, xx,
    grad_s, grad_r, gp_s, gp_r, w_s, w_r, p_s, p_r, kf_s, kf_r, one_s, one_r, two_s, two_r,
    g_s, g_r, f_s, f_r, load,
):
    ctx, ch = lax.axis_index("ctx"), lax.axis_index("ch")
    zl, y, core = ctx // 8, (ctx // 2) % 4, ctx % 2
    chip = ctx // 2
    x, zh = ch % 4, ch // 4
    sib = (chip * 2 + 1 - core, ch)
    far = (ctx, lax.rem(ch + 4, 8))
    z1 = zl + 1 - 2 * (zl % 2)
    z2 = zl + 2 - 4 * ((zl // 2) % 2)
    z4 = lax.rem(zl + 4, 8)

    def place(zz):
        return (zz * 8 + y * 2 + core, ch)

    def remote(src, dst, send, recv, device):
        return pltpu.make_async_remote_copy(
            src_ref=src, dst_ref=dst, send_sem=send, recv_sem=recv, device_id=device, device_id_type=MESH
        )

    def drain(ref, sem):
        pltpu.make_async_copy(ref, ref, sem).wait()

    owed = {}

    def owe(name, ref, sem):
        owed[name] = lambda: drain(ref, sem)

    def settle(*names):
        for name in names or list(owed):
            owed.pop(name)()

    entry = pltpu.get_barrier_semaphore()

    def greet(d, carry):
        pl.semaphore_signal(entry, 1, device_id=(lax.rem(ctx + d, 64), ch), device_id_type=MESH)
        return carry

    lax.fori_loop(1, 64, greet, 0)

    def near(d):
        x_to, y_to = lax.rem(x + d // 4, 4), lax.rem(y + d % 4, 4)
        return x_to, y_to, (zl * 8 + y_to * 2 + core, zh * 4 + x_to)

    def greet_near(d, carry):
        pl.semaphore_signal(entry, 1, device_id=near(d)[2], device_id_type=MESH)
        return carry

    lax.fori_loop(4, 16, greet_near, 0)
    pl.semaphore_signal(entry, 1, device_id=far, device_id_type=MESH)

    pairs = (
        (g_in, g_ref), (w_in, wa.at[zl, core]), (q_in, q_ref), (z_in, z_ref), (k_in, k_ref), (v_in, v_ref), (h_in, h_ref),
        (first_in, first_ref), (swapped_in, swapped_ref), (twist_in, twist_ref), (forth_in, forth_ref),
        (back_in, back_ref), (last_in, last_ref),
    )
    loads = [pltpu.make_async_copy(src, dst, load.at[i]) for i, (src, dst) in enumerate(pairs)]
    for copy in loads:
        copy.start()
    for copy in loads[:7]:
        copy.wait()
    pa[y] = (q_ref[...].astype(F32) * z_ref[...].astype(F32)).astype(BF16)

    def stage_pair(t, carry):
        cols = pl.ds(pl.multiple_of(t * 128, 128), 128)
        kv = (k_ref[:, cols].astype(F32) * v_ref[:, cols].astype(F32)).T.reshape(16, 8, 128)
        filt = h_ref[:, cols].astype(F32).T.reshape(16, 8, 128)
        skf[pl.ds(t * 16, 16)] = jnp.concatenate([kv, filt], axis=1).astype(BF16)
        return carry

    lax.fori_loop(0, 4, stage_pair, 0)
    rkf[ctx] = skf[ctx]
    pl.semaphore_wait(entry, 76)

    far_copy = remote(g_ref, gp, gp_s, gp_r, far)
    far_copy.start()
    owed["far_s"] = far_copy.wait_send
    owed["far_r"] = far_copy.wait_recv
    owe("w_s0", wa.at[0, 0], w_s.at[0])
    owe("w_s1", wa.at[pl.ds(0, 2), 0], w_s.at[1])
    owe("w_s2", wa.at[pl.ds(0, 4), 0], w_s.at[2])
    owe("w_s3", wa.at[:, 0], w_s.at[3])
    owe("w_r3", wa.at[:, 0], w_r.at[3])

    def send_w(block, device, step):
        return remote(wa.at[block, core], wa.at[block, core], w_s.at[step], w_r.at[step], device)

    send_w(zl, place(z4), 0).start()
    send_w(zl, sib, 3).start()

    def spread(src, row, half):
        def body(d, carry):
            x_to, y_to, device = near(d)
            cols = pl.ds(pl.multiple_of(y_to * 128, 128), 128)
            remote(src.at[:, cols], ga.at[row, x * 4 + y], grad_s.at[half], grad_r.at[half], device).start()
            return carry

        lax.fori_loop(1, 16, body, 0)
        owe(f"grad_s{half}", ga.at[0, pl.ds(0, 15)], grad_s.at[half])
        owe(f"grad_r{half}", ga.at[0, pl.ds(0, 15)], grad_r.at[half])
        ga[row, x * 4 + y] = src[:, pl.ds(pl.multiple_of(y * 128, 128), 128)]

    spread(g_ref, zh, 0)
    owe("p_s", pa.at[pl.ds(0, 3)], p_s)
    owe("p_r", pa.at[pl.ds(0, 3)], p_r)
    for d in range(1, 4):
        y_to = lax.rem(y + d, 4)
        remote(pa.at[y], pa.at[y], p_s, p_r, (zl * 8 + y_to * 2 + core, ch)).start()

    drain(wa.at[0, 0], w_r.at[0])
    send_w(zl, place(z2), 1).start()
    send_w(z4, place(z2), 1).start()
    send_w(z4, sib, 3).start()
    drain(wa.at[pl.ds(0, 2), 0], w_r.at[1])
    z24 = lax.rem(z2 + 4, 8)
    for block in (zl, z4, z2, z24):
        send_w(block, place(z1), 2).start()
    send_w(z2, sib, 3).start()
    send_w(z24, sib, 3).start()

    settle("far_r")
    spread(gp, 1 - zh, 1)

    def send_pair(d, carry):
        to = lax.rem(ctx + d, 64)
        remote(skf.at[to], rkf.at[ctx], kf_s, kf_r, (to, ch)).start()
        return carry

    lax.fori_loop(1, 64, send_pair, 0)
    owe("kf_s", skf.at[pl.ds(0, 63)], kf_s)
    owe("kf_r", rkf.at[pl.ds(0, 63)], kf_r)

    drain(wa.at[pl.ds(0, 4), 0], w_r.at[2])
    for block in (z1, lax.rem(z1 + 4, 8), z1 + 2 - 4 * ((z1 // 2) % 2), lax.rem(z1 + 6 - 4 * ((z1 // 2) % 2), 8)):
        send_w(block, sib, 3).start()
    settle("w_r3")
    settle("grad_r0")

    acc1[...] = jnp.zeros_like(acc1)

    def multiply(row):
        def body(t, carry):
            left = ga[row, pl.ds(t * 4, 4)].reshape(512, 128)
            right = wa[row * 4 + t].reshape(128, 512)
            acc1[...] += jnp.dot(left, right, preferred_element_type=F32)
            return carry

        lax.fori_loop(0, 4, body, 0)

    multiply(zh)
    settle("grad_r1")
    multiply(1 - zh)
    owe("one_s", s1, one_s)
    owe("one_r", r1, one_r)
    for d in range(1, 4):
        y_to = lax.rem(y + d, 4)
        s1[d - 1] = acc1[pl.ds(pl.multiple_of(y_to * 128, 128), 128), :].astype(BF16)
        remote(s1.at[d - 1], r1.at[d - 1], one_s, one_r, (zl * 8 + y_to * 2 + core, ch)).start()

    settle("p_r")
    first_core = core == 0

    def partial_rows(t, carry):
        left = ga[t // 4, pl.ds((t % 4) * 4, 4)].reshape(512, 128)
        part = lax.dot_general(
            left, pa[...].reshape(512, 512), (((0,), (0,)), ((), ())), preferred_element_type=F32
        )
        top, low = part[:64], part[64:]
        acc2[t] = jnp.where(first_core, top, low)
        sc[t] = jnp.where(first_core, low, top).astype(BF16)
        return carry

    lax.fori_loop(0, 8, partial_rows, 0)
    core_copy = remote(sc, rc, two_s.at[0], two_r.at[0], sib)
    core_copy.start()
    owed["core_s"], owed["core_r"] = core_copy.wait_send, core_copy.wait_recv

    settle("one_r")
    delta = acc1[pl.ds(pl.multiple_of(y * 128, 128), 128), :]
    for d in range(3):
        delta = delta + r1[d].astype(F32)
    qg_ref[...] = (delta * z_ref[...].astype(F32)).astype(BF16)
    conv = (delta * q_ref[...].astype(F32)).astype(BF16).astype(F32)
    sg[...] = conv.T.reshape(32, 16, 128).astype(BF16)
    rg[core, chip] = sg[chip]

    def send_conv(d, carry):
        to = lax.rem(chip + d, 32)
        remote(sg.at[to], rg.at[core, chip], g_s.at[0], g_r.at[0], (to * 2 + core, ch)).start()
        return carry

    lax.fori_loop(1, 32, send_conv, 0)
    owe("g_s", sg.at[pl.ds(0, 31)], g_s.at[0])
    owe("g_r", rg.at[0, pl.ds(0, 31)], g_r.at[0])

    settle("core_r")
    bit0, bit1, bit2 = zl % 2, (zl // 2) % 2, zl // 4
    for i in range(4):
        give, keep = 2 * i + 1 - bit0, 2 * i + bit0
        sa[i] = (acc2[give] + rc[give].astype(F32)).astype(BF16)
        acc2[keep] = acc2[keep] + rc[keep].astype(F32)
    a_copy = remote(sa, ra, two_s.at[1], two_r.at[1], place(z1))
    a_copy.start()
    owed["a_s"], owed["a_r"] = a_copy.wait_send, a_copy.wait_recv

    for copy in loads[7:]:
        copy.wait()
    twist_cos, twist_sin = twist_ref[0], twist_ref[1]

    def spectrum(base, table, slot):
        for c in range(8):
            dd[:, c * 128 : (c + 1) * 128] = fs[pl.ds(base + c, 64, stride=16), :].astype(BF16)
        both = jnp.dot(table[...], dd[...], preferred_element_type=F32)
        both = both[: 2 * HALF] + both[2 * HALF :]
        for c in range(8):
            real = both[:HALF, c * 128 : (c + 1) * 128]
            imag = both[HALF:, c * 128 : (c + 1) * 128]
            aa[c * HALF : (c + 1) * HALF, :128] = real * twist_cos + imag * twist_sin
            aa[c * HALF : (c + 1) * HALF, 128:] = imag * twist_cos - real * twist_sin
        spec[slot] = three(aa[...], forth_ref[0], forth_ref[1])

    settle("kf_r")
    fs[...] = rkf[...].astype(F32).reshape(1024, 128)
    spectrum(0, first_ref, 0)
    spectrum(8, first_ref, 1)

    settle("a_r")
    for i in range(2):
        give, keep = 2 * i + 1 - bit1, 2 * i + bit1
        sb[i] = (acc2[2 * give + bit0] + ra[give].astype(F32)).astype(BF16)
        acc2[2 * keep + bit0] = acc2[2 * keep + bit0] + ra[keep].astype(F32)
    b_copy = remote(sb, rb, two_s.at[2], two_r.at[2], place(z2))
    b_copy.start()
    owed["b_s"], owed["b_r"] = b_copy.wait_send, b_copy.wait_recv

    settle("g_r")
    g_copy = remote(rg.at[core], rg.at[core], g_s.at[1], g_r.at[1], sib)
    g_copy.start()
    owed["gs_s"], owed["gs_r"] = g_copy.wait_send, g_copy.wait_recv

    settle("b_r")
    give, keep = 1 - bit2, bit2
    sd[...] = (acc2[4 * give + 2 * bit1 + bit0] + rb[give].astype(F32)).astype(BF16)
    d_copy = remote(sd, rd, two_s.at[3], two_r.at[3], place(z4))
    d_copy.start()
    owed["d_s"], owed["d_r"] = d_copy.wait_send, d_copy.wait_recv
    mine = acc2[4 * keep + 2 * bit1 + bit0] + rb[keep].astype(F32)
    wg_ref[...] = mine

    settle("gs_r")
    fs[...] = rg[...].astype(F32).reshape(1024, 128)
    spectrum(core * 8, swapped_ref, 2)

    for slot, base in ((1, 0), (0, 8)):
        other_real, other_imag = spec[slot, :, :128], spec[slot, :, 128:]
        grad_real, grad_imag = spec[2, :, :128], spec[2, :, 128:]
        aa[:, :128] = other_real * grad_real + other_imag * grad_imag
        aa[:, 128:] = other_real * grad_imag - other_imag * grad_real
        turned = three(aa[...], back_ref[0], back_ref[1])
        for c in range(8):
            real = turned[c * HALF : (c + 1) * HALF, :128]
            imag = turned[c * HALF : (c + 1) * HALF, 128:]
            xx[:HALF, c * 128 : (c + 1) * 128] = real * twist_cos - imag * twist_sin
            xx[HALF:, c * 128 : (c + 1) * 128] = real * twist_sin + imag * twist_cos
        right = xx[...]
        right_high = right.astype(BF16)
        right_low = (right - right_high.astype(F32)).astype(BF16)
        signal = (
            jnp.dot(last_ref[0], right_high, preferred_element_type=F32)
            + jnp.dot(last_ref[0], right_low, preferred_element_type=F32)
            + jnp.dot(last_ref[1], right_high, preferred_element_type=F32)
        )
        for c in range(8):
            fs[pl.ds(base + c, 64, stride=16), :] = signal[:, c * 128 : (c + 1) * 128]
    sf[...] = fs[...].astype(BF16).reshape(64, 16, 128)
    rf[ctx] = sf[ctx]

    def send_back(d, carry):
        to = lax.rem(ctx + d, 64)
        remote(sf.at[to], rf.at[ctx], f_s, f_r, (to, ch)).start()
        return carry

    lax.fori_loop(1, 64, send_back, 0)
    owe("f_s", sf.at[pl.ds(0, 63)], f_s)
    owe("f_r", rf.at[pl.ds(0, 63)], f_r)

    settle("d_r")
    wg_ref[...] = wg_ref[...] + rd[...].astype(F32)

    settle("f_r")
    for t in range(4):
        back = rf[t * 16 : (t + 1) * 16].astype(F32)
        vd_ref[:, t * 128 : (t + 1) * 128] = back[:, :8].reshape(128, 128).T.astype(BF16)
        fg_ref[:, t * 128 : (t + 1) * 128] = back[:, 8:].reshape(128, 128).T.astype(BF16)
    settle()


def on_device(
    queries, keys, values, conv_out, filters, out_grad, out_weight, moment_one, moment_two
):
    tables = [jnp.asarray(t) for t in dft_tables()]
    vmem = pl.BlockSpec(memory_space=pltpu.VMEM)
    dma = pltpu.SemaphoreType.DMA

    def half(*shape):
        return pltpu.VMEM(shape, BF16)

    def full(*shape):
        return pltpu.VMEM(shape, F32)

    query_grad, value_delta, filter_grad, weight_grad = pl.pallas_call(
        kernel,
        out_shape=(
            jax.ShapeDtypeStruct((128, 512), BF16),
            jax.ShapeDtypeStruct((128, 512), BF16),
            jax.ShapeDtypeStruct((128, 512), BF16),
            jax.ShapeDtypeStruct((64, 512), F32),
        ),
        in_specs=[pl.BlockSpec(memory_space=pltpu.HBM)] * 13,
        out_specs=(vmem,) * 4,
        scratch_shapes=[
            *[half(128, 512)] * 6,
            *[pltpu.VMEM(t.shape, t.dtype) for t in tables],
            half(2, 16, 128, 128),
            half(128, 512),
            half(8, 2, 64, 512),
            half(4, 128, 512),
            half(64, 16, 128),
            half(64, 16, 128),
            half(3, 128, 512),
            half(3, 128, 512),
            full(512, 512),
            half(8, 64, 512),
            half(8, 64, 512),
            full(8, 64, 512),
            half(4, 64, 512),
            half(4, 64, 512),
            half(2, 64, 512),
            half(2, 64, 512),
            half(64, 512),
            half(64, 512),
            half(32, 16, 128),
            half(2, 32, 16, 128),
            half(64, 16, 128),
            half(64, 16, 128),
            full(1024, 128),
            half(64, 1024),
            full(8 * HALF, 256),
            full(3, 8 * HALF, 256),
            full(2 * HALF, 1024),
            dma((2,)), dma((2,)),
            dma, dma,
            dma((4,)), dma((4,)),
            dma, dma,
            dma, dma,
            dma, dma,
            dma((4,)), dma((4,)),
            dma((2,)), dma((2,)),
            dma, dma,
            dma((13,)),
        ],
        compiler_params=pltpu.CompilerParams(
            collective_id=1, has_side_effects=True, vmem_limit_bytes=60 * 2**20
        ),
    )(queries, keys, values, conv_out, filters, out_grad, out_weight, *tables)

    delta = value_delta.astype(F32)
    key_grad = (delta * values.astype(F32)).astype(BF16)
    value_grad = (delta * keys.astype(F32)).astype(BF16)
    new_moment_one = BETA_ONE * moment_one + (1.0 - BETA_ONE) * weight_grad
    new_moment_two = BETA_TWO * moment_two + (1.0 - BETA_TWO) * weight_grad * weight_grad
    corr_one = 1.0 - BETA_ONE**10
    corr_two = 1.0 - BETA_TWO**10
    weight_float = out_weight.astype(F32)
    update = new_moment_one / corr_one / (jnp.sqrt(new_moment_two / corr_two) + ADAM_STABILIZER)
    new_weight = (weight_float - STEP_RATE * (update + DECAY * weight_float)).astype(BF16)
    return (
        query_grad,
        key_grad,
        value_grad,
        filter_grad,
        new_weight,
        new_moment_one,
        new_moment_two,
    )


def solution(mesh):
    spec = P("ctx", "ch")
    return jax.shard_map(
        on_device, mesh=mesh, in_specs=(spec,) * 9, out_specs=(spec,) * 7, check_vma=False
    )
```

```python
import math

import jax
import jax.numpy as jnp
import numpy as np
from jax import lax
from jax.experimental import pallas as pl
from jax.experimental.pallas import tpu as pltpu
from jax.sharding import PartitionSpec as P

BETA_ONE = 0.9
BETA_TWO = 0.95
STEP_RATE = 0.003
DECAY = 0.1
ADAM_STABILIZER = 1e-08

MESH = pl.DeviceIdType.MESH
F32 = jnp.float32
BF16 = jnp.bfloat16
HALF = 72


def halves(table):
    high = table.astype(np.float32).astype(BF16)
    low = (table.astype(np.float32) - high.astype(np.float32)).astype(BF16)
    return high, low


def dft_tables():
    k = np.arange(HALF)[:, None]
    j = np.arange(64)[None, :]
    outer = 2.0 * math.pi * ((k * j) % 128) / 128
    first = np.concatenate([np.cos(outer), -np.sin(outer)], axis=0)
    first = np.concatenate(halves(first), axis=0)
    swapped = np.concatenate([first[:, 0::2], first[:, 1::2]], axis=1)
    m = np.arange(128)[None, :]
    turn = 2.0 * math.pi * (k * m) / 16384
    twist = np.stack([np.cos(turn), np.sin(turn)]).astype(np.float32)
    inner = 2.0 * math.pi * ((np.arange(128)[:, None] * m) % 128) / 128
    c, s = np.cos(inner), np.sin(inner)
    forth = np.stack(halves(np.block([[c, -s], [s, c]])))
    back = np.stack(halves(np.block([[c, s], [-s, c]])))
    weight = np.where((k == 0) | (k == 64), 1.0, np.where(k < 64, 2.0, 0.0)) / 16384
    last = np.concatenate([weight * np.cos(outer), -weight * np.sin(outer)], axis=0).T
    last = np.stack(halves(last))
    return first, swapped, twist, forth, back, last


def three(left, high, low):
    left_high = left.astype(BF16)
    left_low = (left - left_high.astype(F32)).astype(BF16)
    return (
        jnp.dot(left_high, high, preferred_element_type=F32)
        + jnp.dot(left_low, high, preferred_element_type=F32)
        + jnp.dot(left_high, low, preferred_element_type=F32)
    )


def kernel(
    q_in, k_in, v_in, z_in, h_in, g_in, w_in,
    first_in, swapped_in, twist_in, forth_in, back_in, last_in,
    qg_ref, vd_ref, fg_ref, wg_ref,
    q_ref, k_ref, v_ref, z_ref, h_ref, g_ref,
    first_ref, swapped_ref, twist_ref, forth_ref, back_ref, last_ref,
    ga, gp, wa, pa, skf, rkf, s1, r1, acc1, sc, rc, acc2, sa, ra, sb, rb, sd, rd,
    sg, rg, sf, rf, fs, dd, aa, spec, xx,
    grad_s, grad_r, gp_s, gp_r, w_s, w_r, p_s, p_r, kf_s, kf_r, one_s, one_r, two_s, two_r,
    g_s, g_r, f_s, f_r, load,
):
    ctx, ch = lax.axis_index("ctx"), lax.axis_index("ch")
    zl, y, core = ctx // 8, (ctx // 2) % 4, ctx % 2
    chip = ctx // 2
    x, zh = ch % 4, ch // 4
    sib = (chip * 2 + 1 - core, ch)
    far = (ctx, lax.rem(ch + 4, 8))
    z1 = zl + 1 - 2 * (zl % 2)
    z2 = zl + 2 - 4 * ((zl // 2) % 2)
    z4 = lax.rem(zl + 4, 8)

    def place(zz):
        return (zz * 8 + y * 2 + core, ch)

    def remote(src, dst, send, recv, device):
        return pltpu.make_async_remote_copy(
            src_ref=src, dst_ref=dst, send_sem=send, recv_sem=recv, device_id=device, device_id_type=MESH
        )

    def drain(ref, sem):
        pltpu.make_async_copy(ref, ref, sem).wait()

    owed = {}

    def owe(name, ref, sem):
        owed[name] = lambda: drain(ref, sem)

    def settle(*names):
        for name in names or list(owed):
            owed.pop(name)()

    entry = pltpu.get_barrier_semaphore()

    def greet(d, carry):
        pl.semaphore_signal(entry, 1, device_id=(lax.rem(ctx + d, 64), ch), device_id_type=MESH)
        return carry

    lax.fori_loop(1, 64, greet, 0)

    def near(d):
        x_to, y_to = lax.rem(x + d // 4, 4), lax.rem(y + d % 4, 4)
        return x_to, y_to, (zl * 8 + y_to * 2 + core, zh * 4 + x_to)

    def greet_near(d, carry):
        pl.semaphore_signal(entry, 1, device_id=near(d)[2], device_id_type=MESH)
        return carry

    lax.fori_loop(4, 16, greet_near, 0)
    pl.semaphore_signal(entry, 1, device_id=far, device_id_type=MESH)

    pairs = (
        (g_in, g_ref), (w_in, wa.at[zl, core]), (q_in, q_ref), (z_in, z_ref), (k_in, k_ref), (v_in, v_ref), (h_in, h_ref),
        (first_in, first_ref), (swapped_in, swapped_ref), (twist_in, twist_ref), (forth_in, forth_ref),
        (back_in, back_ref), (last_in, last_ref),
    )
    loads = [pltpu.make_async_copy(src, dst, load.at[i]) for i, (src, dst) in enumerate(pairs)]
    for copy in loads:
        copy.start()
    loads[0].wait()
    loads[1].wait()
    pl.semaphore_wait(entry, 76)

    owe("w_s0", wa.at[0, 0], w_s.at[0])
    owe("w_s1", wa.at[pl.ds(0, 2), 0], w_s.at[1])
    owe("w_s2", wa.at[pl.ds(0, 4), 0], w_s.at[2])
    owe("w_s3", wa.at[:, 0], w_s.at[3])
    owe("w_r3", wa.at[:, 0], w_r.at[3])

    def send_w(block, device, step):
        return remote(wa.at[block, core], wa.at[block, core], w_s.at[step], w_r.at[step], device)

    send_w(zl, place(z4), 0).start()
    send_w(zl, sib, 3).start()

    far_copies = []
    for i in range(4):
        cols = pl.ds(pl.multiple_of(lax.rem(y + 1 + i, 4) * 128, 128), 128)
        far_copies.append(remote(g_ref.at[:, cols], gp.at[:, cols], gp_s.at[i], gp_r.at[i], far))
        far_copies[i].start()
        owed[f"far_s{i}"] = far_copies[i].wait_send
        owed[f"far_r{i}"] = far_copies[i].wait_recv

    def spread(src, row, half, i):
        y_to = lax.rem(y + 1 + i, 4)
        cols = pl.ds(pl.multiple_of(y_to * 128, 128), 128)
        for d in range(4):
            x_to = lax.rem(x + d, 4)
            if d or i < 3:
                device = (zl * 8 + y_to * 2 + core, zh * 4 + x_to)
                remote(src.at[:, cols], ga.at[row, x * 4 + y], grad_s.at[half], grad_r.at[half], device).start()
            else:
                ga[row, x * 4 + y] = src[:, cols]
        if i == 3:
            owe(f"grad_s{half}", ga.at[0, pl.ds(0, 15)], grad_s.at[half])
            owe(f"grad_r{half}", ga.at[0, pl.ds(0, 15)], grad_r.at[half])

    for i in range(4):
        spread(g_ref, zh, 0, i)

    loads[2].wait()
    loads[3].wait()
    pa[y] = (q_ref[...].astype(F32) * z_ref[...].astype(F32)).astype(BF16)
    owe("p_s", pa.at[pl.ds(0, 3)], p_s)
    owe("p_r", pa.at[pl.ds(0, 3)], p_r)
    for d in range(1, 4):
        y_to = lax.rem(y + d, 4)
        remote(pa.at[y], pa.at[y], p_s, p_r, (zl * 8 + y_to * 2 + core, ch)).start()

    drain(wa.at[0, 0], w_r.at[0])
    send_w(zl, place(z2), 1).start()
    send_w(z4, place(z2), 1).start()
    send_w(z4, sib, 3).start()

    for copy in loads[4:7]:
        copy.wait()

    def stage_pair(t, carry):
        cols = pl.ds(pl.multiple_of(t * 128, 128), 128)
        kv = (k_ref[:, cols].astype(F32) * v_ref[:, cols].astype(F32)).T.reshape(16, 8, 128)
        filt = h_ref[:, cols].astype(F32).T.reshape(16, 8, 128)
        skf[pl.ds(t * 16, 16)] = jnp.concatenate([kv, filt], axis=1).astype(BF16)
        return carry

    lax.fori_loop(0, 4, stage_pair, 0)
    rkf[ctx] = skf[ctx]

    def send_pair(d, carry):
        to = lax.rem(ctx + d, 64)
        remote(skf.at[to], rkf.at[ctx], kf_s, kf_r, (to, ch)).start()
        return carry

    lax.fori_loop(1, 64, send_pair, 0)
    owe("kf_s", skf.at[pl.ds(0, 63)], kf_s)
    owe("kf_r", rkf.at[pl.ds(0, 63)], kf_r)
    for i in range(2):
        settle(f"far_r{i}")
        spread(gp, 1 - zh, 1, i)

    drain(wa.at[pl.ds(0, 2), 0], w_r.at[1])
    z24 = lax.rem(z2 + 4, 8)
    for block in (zl, z4, z2, z24):
        send_w(block, place(z1), 2).start()
    send_w(z2, sib, 3).start()
    send_w(z24, sib, 3).start()

    for i in range(2, 4):
        settle(f"far_r{i}")
        spread(gp, 1 - zh, 1, i)

    settle("grad_r0", "grad_r1")

    settle("p_r")
    first_core = core == 0

    def partial_rows(t, carry):
        left = ga[t // 4, pl.ds((t % 4) * 4, 4)].reshape(512, 128)
        part = lax.dot_general(
            left, pa[...].reshape(512, 512), (((0,), (0,)), ((), ())), preferred_element_type=F32
        )
        top, low = part[:64], part[64:]
        acc2[t] = jnp.where(first_core, top, low)
        sc[t] = jnp.where(first_core, low, top).astype(BF16)
        return carry

    lax.fori_loop(0, 8, partial_rows, 0)
    core_copy = remote(sc, rc, two_s.at[0], two_r.at[0], sib)
    core_copy.start()
    owed["core_s"], owed["core_r"] = core_copy.wait_send, core_copy.wait_recv

    drain(wa.at[pl.ds(0, 4), 0], w_r.at[2])
    for block in (z1, lax.rem(z1 + 4, 8), z1 + 2 - 4 * ((z1 // 2) % 2), lax.rem(z1 + 6 - 4 * ((z1 // 2) % 2), 8)):
        send_w(block, sib, 3).start()

    settle("core_r")
    bit0, bit1, bit2 = zl % 2, (zl // 2) % 2, zl // 4
    for i in range(4):
        give, keep = 2 * i + 1 - bit0, 2 * i + bit0
        sa[i] = (acc2[give] + rc[give].astype(F32)).astype(BF16)
        acc2[keep] = acc2[keep] + rc[keep].astype(F32)
    a_copy = remote(sa, ra, two_s.at[1], two_r.at[1], place(z1))
    a_copy.start()
    owed["a_s"], owed["a_r"] = a_copy.wait_send, a_copy.wait_recv

    settle("w_r3")

    acc1[...] = jnp.zeros_like(acc1)

    def multiply(row):
        def body(t, carry):
            left = ga[row, pl.ds(t * 4, 4)].reshape(512, 128)
            right = wa[row * 4 + t].reshape(128, 512)
            acc1[...] += jnp.dot(left, right, preferred_element_type=F32)
            return carry

        lax.fori_loop(0, 4, body, 0)

    multiply(zh)
    multiply(1 - zh)
    owe("one_s", s1, one_s)
    owe("one_r", r1, one_r)
    for d in range(1, 4):
        y_to = lax.rem(y + d, 4)
        s1[d - 1] = acc1[pl.ds(pl.multiple_of(y_to * 128, 128), 128), :].astype(BF16)
        remote(s1.at[d - 1], r1.at[d - 1], one_s, one_r, (zl * 8 + y_to * 2 + core, ch)).start()


    settle("a_r")
    for i in range(2):
        give, keep = 2 * i + 1 - bit1, 2 * i + bit1
        sb[i] = (acc2[2 * give + bit0] + ra[give].astype(F32)).astype(BF16)
        acc2[2 * keep + bit0] = acc2[2 * keep + bit0] + ra[keep].astype(F32)
    b_copy = remote(sb, rb, two_s.at[2], two_r.at[2], place(z2))
    b_copy.start()
    owed["b_s"], owed["b_r"] = b_copy.wait_send, b_copy.wait_recv

    settle("one_r")
    delta = acc1[pl.ds(pl.multiple_of(y * 128, 128), 128), :]
    for d in range(3):
        delta = delta + r1[d].astype(F32)
    qg_ref[...] = (delta * z_ref[...].astype(F32)).astype(BF16)
    conv = (delta * q_ref[...].astype(F32)).astype(BF16).astype(F32)
    sg[...] = conv.T.reshape(32, 16, 128).astype(BF16)
    rg[core, chip] = sg[chip]

    def send_conv(d, carry):
        to = lax.rem(chip + d, 32)
        remote(sg.at[to], rg.at[core, chip], g_s.at[0], g_r.at[0], (to * 2 + core, ch)).start()
        return carry

    lax.fori_loop(1, 32, send_conv, 0)
    owe("g_s", sg.at[pl.ds(0, 31)], g_s.at[0])
    owe("g_r", rg.at[0, pl.ds(0, 31)], g_r.at[0])

    settle("b_r")
    give, keep = 1 - bit2, bit2
    sd[...] = (acc2[4 * give + 2 * bit1 + bit0] + rb[give].astype(F32)).astype(BF16)
    d_copy = remote(sd, rd, two_s.at[3], two_r.at[3], place(z4))
    d_copy.start()
    owed["d_s"], owed["d_r"] = d_copy.wait_send, d_copy.wait_recv
    mine = acc2[4 * keep + 2 * bit1 + bit0] + rb[keep].astype(F32)
    wg_ref[...] = mine

    for copy in loads[7:]:
        copy.wait()
    twist_cos, twist_sin = twist_ref[0], twist_ref[1]

    def spectrum(base, table, slot):
        for c in range(8):
            dd[:, c * 128 : (c + 1) * 128] = fs[pl.ds(base + c, 64, stride=16), :].astype(BF16)
        both = jnp.dot(table[...], dd[...], preferred_element_type=F32)
        both = both[: 2 * HALF] + both[2 * HALF :]
        for c in range(8):
            real = both[:HALF, c * 128 : (c + 1) * 128]
            imag = both[HALF:, c * 128 : (c + 1) * 128]
            aa[c * HALF : (c + 1) * HALF, :128] = real * twist_cos + imag * twist_sin
            aa[c * HALF : (c + 1) * HALF, 128:] = imag * twist_cos - real * twist_sin
        spec[slot] = three(aa[...], forth_ref[0], forth_ref[1])

    settle("kf_r")
    fs[...] = rkf[...].astype(F32).reshape(1024, 128)
    spectrum(0, first_ref, 0)
    spectrum(8, first_ref, 1)

    settle("g_r")
    g_copy = remote(rg.at[core], rg.at[core], g_s.at[1], g_r.at[1], sib)
    g_copy.start()
    owed["gs_s"], owed["gs_r"] = g_copy.wait_send, g_copy.wait_recv

    settle("gs_r")
    fs[...] = rg[...].astype(F32).reshape(1024, 128)
    spectrum(core * 8, swapped_ref, 2)

    for slot, base in ((1, 0), (0, 8)):
        other_real, other_imag = spec[slot, :, :128], spec[slot, :, 128:]
        grad_real, grad_imag = spec[2, :, :128], spec[2, :, 128:]
        aa[:, :128] = other_real * grad_real + other_imag * grad_imag
        aa[:, 128:] = other_real * grad_imag - other_imag * grad_real
        turned = three(aa[...], back_ref[0], back_ref[1])
        for c in range(8):
            real = turned[c * HALF : (c + 1) * HALF, :128]
            imag = turned[c * HALF : (c + 1) * HALF, 128:]
            xx[:HALF, c * 128 : (c + 1) * 128] = real * twist_cos - imag * twist_sin
            xx[HALF:, c * 128 : (c + 1) * 128] = real * twist_sin + imag * twist_cos
        right = xx[...]
        right_high = right.astype(BF16)
        right_low = (right - right_high.astype(F32)).astype(BF16)
        signal = (
            jnp.dot(last_ref[0], right_high, preferred_element_type=F32)
            + jnp.dot(last_ref[0], right_low, preferred_element_type=F32)
            + jnp.dot(last_ref[1], right_high, preferred_element_type=F32)
        )
        for c in range(8):
            fs[pl.ds(base + c, 64, stride=16), :] = signal[:, c * 128 : (c + 1) * 128]
    sf[...] = fs[...].astype(BF16).reshape(64, 16, 128)
    rf[ctx] = sf[ctx]

    def send_back(d, carry):
        to = lax.rem(ctx + d, 64)
        remote(sf.at[to], rf.at[ctx], f_s, f_r, (to, ch)).start()
        return carry

    lax.fori_loop(1, 64, send_back, 0)
    owe("f_s", sf.at[pl.ds(0, 63)], f_s)
    owe("f_r", rf.at[pl.ds(0, 63)], f_r)

    settle("d_r")
    wg_ref[...] = wg_ref[...] + rd[...].astype(F32)

    settle("f_r")
    for t in range(4):
        back = rf[t * 16 : (t + 1) * 16].astype(F32)
        vd_ref[:, t * 128 : (t + 1) * 128] = back[:, :8].reshape(128, 128).T.astype(BF16)
        fg_ref[:, t * 128 : (t + 1) * 128] = back[:, 8:].reshape(128, 128).T.astype(BF16)
    settle()


def on_device(
    queries, keys, values, conv_out, filters, out_grad, out_weight, moment_one, moment_two
):
    tables = [jnp.asarray(t) for t in dft_tables()]
    vmem = pl.BlockSpec(memory_space=pltpu.VMEM)
    dma = pltpu.SemaphoreType.DMA

    def half(*shape):
        return pltpu.VMEM(shape, BF16)

    def full(*shape):
        return pltpu.VMEM(shape, F32)

    query_grad, value_delta, filter_grad, weight_grad = pl.pallas_call(
        kernel,
        out_shape=(
            jax.ShapeDtypeStruct((128, 512), BF16),
            jax.ShapeDtypeStruct((128, 512), BF16),
            jax.ShapeDtypeStruct((128, 512), BF16),
            jax.ShapeDtypeStruct((64, 512), F32),
        ),
        in_specs=[pl.BlockSpec(memory_space=pltpu.HBM)] * 13,
        out_specs=(vmem,) * 4,
        scratch_shapes=[
            *[half(128, 512)] * 6,
            *[pltpu.VMEM(t.shape, t.dtype) for t in tables],
            half(2, 16, 128, 128),
            half(128, 512),
            half(8, 2, 64, 512),
            half(4, 128, 512),
            half(64, 16, 128),
            half(64, 16, 128),
            half(3, 128, 512),
            half(3, 128, 512),
            full(512, 512),
            half(8, 64, 512),
            half(8, 64, 512),
            full(8, 64, 512),
            half(4, 64, 512),
            half(4, 64, 512),
            half(2, 64, 512),
            half(2, 64, 512),
            half(64, 512),
            half(64, 512),
            half(32, 16, 128),
            half(2, 32, 16, 128),
            half(64, 16, 128),
            half(64, 16, 128),
            full(1024, 128),
            half(64, 1024),
            full(8 * HALF, 256),
            full(3, 8 * HALF, 256),
            full(2 * HALF, 1024),
            dma((2,)), dma((2,)),
            dma((4,)), dma((4,)),
            dma((4,)), dma((4,)),
            dma, dma,
            dma, dma,
            dma, dma,
            dma((4,)), dma((4,)),
            dma((2,)), dma((2,)),
            dma, dma,
            dma((13,)),
        ],
        compiler_params=pltpu.CompilerParams(
            collective_id=1, has_side_effects=True, vmem_limit_bytes=60 * 2**20
        ),
    )(queries, keys, values, conv_out, filters, out_grad, out_weight, *tables)

    delta = value_delta.astype(F32)
    key_grad = (delta * values.astype(F32)).astype(BF16)
    value_grad = (delta * keys.astype(F32)).astype(BF16)
    new_moment_one = BETA_ONE * moment_one + (1.0 - BETA_ONE) * weight_grad
    new_moment_two = BETA_TWO * moment_two + (1.0 - BETA_TWO) * weight_grad * weight_grad
    corr_one = 1.0 - BETA_ONE**10
    corr_two = 1.0 - BETA_TWO**10
    weight_float = out_weight.astype(F32)
    update = new_moment_one / corr_one / (jnp.sqrt(new_moment_two / corr_two) + ADAM_STABILIZER)
    new_weight = (weight_float - STEP_RATE * (update + DECAY * weight_float)).astype(BF16)
    return (
        query_grad,
        key_grad,
        value_grad,
        filter_grad,
        new_weight,
        new_moment_one,
        new_moment_two,
    )


def solution(mesh):
    spec = P("ctx", "ch")
    return jax.shard_map(
        on_device, mesh=mesh, in_specs=(spec,) * 9, out_specs=(spec,) * 7, check_vma=False
    )
```

```python
import math

import jax
import jax.numpy as jnp
import numpy as np
from jax import lax
from jax.experimental import pallas as pl
from jax.experimental.pallas import tpu as pltpu
from jax.sharding import PartitionSpec as P

BETA_ONE = 0.9
BETA_TWO = 0.95
STEP_RATE = 0.003
DECAY = 0.1
ADAM_STABILIZER = 1e-08

MESH = pl.DeviceIdType.MESH
F32 = jnp.float32
BF16 = jnp.bfloat16
HALF = 72


def halves(table):
    high = table.astype(np.float32).astype(BF16)
    low = (table.astype(np.float32) - high.astype(np.float32)).astype(BF16)
    return high, low


def dft_tables():
    k = np.arange(HALF)[:, None]
    j = np.arange(64)[None, :]
    outer = 2.0 * math.pi * ((k * j) % 128) / 128
    first = np.concatenate([np.cos(outer), -np.sin(outer)], axis=0)
    first = np.concatenate(halves(first), axis=0)
    swapped = np.concatenate([first[:, 0::2], first[:, 1::2]], axis=1)
    m = np.arange(128)[None, :]
    turn = 2.0 * math.pi * (k * m) / 16384
    twist = np.stack([np.cos(turn), np.sin(turn)]).astype(np.float32)
    inner = 2.0 * math.pi * ((np.arange(128)[:, None] * m) % 128) / 128
    c, s = np.cos(inner), np.sin(inner)
    forth = np.stack(halves(np.block([[c, -s], [s, c]])))
    back = np.stack(halves(np.block([[c, s], [-s, c]])))
    weight = np.where((k == 0) | (k == 64), 1.0, np.where(k < 64, 2.0, 0.0)) / 16384
    last = np.concatenate([weight * np.cos(outer), -weight * np.sin(outer)], axis=0).T
    last = np.stack(halves(last))
    return first, swapped, twist, forth, back, last


def three(left, high, low):
    left_high = left.astype(BF16)
    left_low = (left - left_high.astype(F32)).astype(BF16)
    return (
        jnp.dot(left_high, high, preferred_element_type=F32)
        + jnp.dot(left_low, high, preferred_element_type=F32)
        + jnp.dot(left_high, low, preferred_element_type=F32)
    )


def kernel(
    q_in, k_in, v_in, z_in, h_in, g_in, w_in,
    first_in, swapped_in, twist_in, forth_in, back_in, last_in,
    qg_ref, vd_ref, fg_ref, wg_ref,
    q_ref, k_ref, v_ref, z_ref, h_ref, g_ref,
    first_ref, swapped_ref, twist_ref, forth_ref, back_ref, last_ref,
    ga, gp, wa, pa, skf, rkf, s1, r1, acc1, sc, rc, acc2, sa, ra, sb, rb, sd, rd,
    sg, rg, sf, rf, fs, dd, aa, spec, xx,
    grad_s, grad_r, gp_s, gp_r, w_s, w_r, p_s, p_r, kf_s, kf_r, one_s, one_r, two_s, two_r,
    g_s, g_r, f_s, f_r, load,
):
    ctx, ch = lax.axis_index("ctx"), lax.axis_index("ch")
    zl, y, core = ctx // 8, (ctx // 2) % 4, ctx % 2
    chip = ctx // 2
    x, zh = ch % 4, ch // 4
    sib = (chip * 2 + 1 - core, ch)
    far = (ctx, lax.rem(ch + 4, 8))
    z1 = zl + 1 - 2 * (zl % 2)
    z2 = zl + 2 - 4 * ((zl // 2) % 2)
    z4 = lax.rem(zl + 4, 8)

    def place(zz):
        return (zz * 8 + y * 2 + core, ch)

    def remote(src, dst, send, recv, device):
        return pltpu.make_async_remote_copy(
            src_ref=src, dst_ref=dst, send_sem=send, recv_sem=recv, device_id=device, device_id_type=MESH
        )

    def drain(ref, sem):
        pltpu.make_async_copy(ref, ref, sem).wait()

    owed = {}

    def owe(name, ref, sem):
        owed[name] = lambda: drain(ref, sem)

    def settle(*names):
        for name in names or list(owed):
            owed.pop(name)()

    entry = pltpu.get_barrier_semaphore()

    def greet(d, carry):
        pl.semaphore_signal(entry, 1, device_id=(lax.rem(ctx + d, 64), ch), device_id_type=MESH)
        return carry

    lax.fori_loop(1, 64, greet, 0)

    def near(d):
        x_to, y_to = lax.rem(x + d // 4, 4), lax.rem(y + d % 4, 4)
        return x_to, y_to, (zl * 8 + y_to * 2 + core, zh * 4 + x_to)

    def greet_near(d, carry):
        pl.semaphore_signal(entry, 1, device_id=near(d)[2], device_id_type=MESH)
        return carry

    lax.fori_loop(4, 16, greet_near, 0)
    pl.semaphore_signal(entry, 1, device_id=far, device_id_type=MESH)

    pairs = (
        (g_in, g_ref), (w_in, wa.at[zl, core]), (q_in, q_ref), (z_in, z_ref), (k_in, k_ref), (v_in, v_ref), (h_in, h_ref),
        (first_in, first_ref), (swapped_in, swapped_ref), (twist_in, twist_ref), (forth_in, forth_ref),
        (back_in, back_ref), (last_in, last_ref),
    )
    loads = [pltpu.make_async_copy(src, dst, load.at[i]) for i, (src, dst) in enumerate(pairs)]
    for copy in loads:
        copy.start()
    loads[0].wait()
    loads[1].wait()
    pl.semaphore_wait(entry, 76)

    owe("w_s0", wa.at[0, 0], w_s.at[0])
    owe("w_s1", wa.at[pl.ds(0, 2), 0], w_s.at[1])
    owe("w_s2", wa.at[pl.ds(0, 4), 0], w_s.at[2])
    owe("w_s3", wa.at[:, 0], w_s.at[3])
    owe("w_r3", wa.at[:, 0], w_r.at[3])

    def send_w(block, device, step):
        return remote(wa.at[block, core], wa.at[block, core], w_s.at[step], w_r.at[step], device)

    send_w(zl, place(z4), 0).start()
    send_w(zl, sib, 3).start()

    far_copies = []
    for i in range(4):
        cols = pl.ds(pl.multiple_of(lax.rem(y + 1 + i, 4) * 128, 128), 128)
        far_copies.append(remote(g_ref.at[:, cols], gp.at[:, cols], gp_s.at[i], gp_r.at[i], far))
        far_copies[i].start()
        owed[f"far_s{i}"] = far_copies[i].wait_send
        owed[f"far_r{i}"] = far_copies[i].wait_recv

    def spread(src, row, half, i):
        y_to = lax.rem(y + 1 + i, 4)
        cols = pl.ds(pl.multiple_of(y_to * 128, 128), 128)
        for d in range(4):
            x_to = lax.rem(x + d, 4)
            if d or i < 3:
                device = (zl * 8 + y_to * 2 + core, zh * 4 + x_to)
                remote(src.at[:, cols], ga.at[row, x * 4 + y], grad_s.at[half], grad_r.at[half], device).start()
            else:
                ga[row, x * 4 + y] = src[:, cols]
        if i == 3:
            owe(f"grad_s{half}", ga.at[0, pl.ds(0, 15)], grad_s.at[half])
            owe(f"grad_r{half}", ga.at[0, pl.ds(0, 15)], grad_r.at[half])

    for i in range(4):
        spread(g_ref, zh, 0, i)

    loads[2].wait()
    loads[3].wait()
    pa[y] = (q_ref[...].astype(F32) * z_ref[...].astype(F32)).astype(BF16)
    owe("p_s", pa.at[pl.ds(0, 3)], p_s)
    owe("p_r", pa.at[pl.ds(0, 3)], p_r)
    for d in range(1, 4):
        y_to = lax.rem(y + d, 4)
        remote(pa.at[y], pa.at[y], p_s, p_r, (zl * 8 + y_to * 2 + core, ch)).start()

    drain(wa.at[0, 0], w_r.at[0])
    send_w(zl, place(z2), 1).start()
    send_w(z4, place(z2), 1).start()
    send_w(z4, sib, 3).start()

    for copy in loads[4:7]:
        copy.wait()

    def stage_pair(t, carry):
        cols = pl.ds(pl.multiple_of(t * 128, 128), 128)
        kv = (k_ref[:, cols].astype(F32) * v_ref[:, cols].astype(F32)).T.reshape(16, 8, 128)
        filt = h_ref[:, cols].astype(F32).T.reshape(16, 8, 128)
        skf[pl.ds(t * 16, 16)] = jnp.concatenate([kv, filt], axis=1).astype(BF16)
        return carry

    lax.fori_loop(0, 4, stage_pair, 0)
    rkf[ctx] = skf[ctx]

    def send_pair(d, carry):
        to = lax.rem(ctx + d, 64)
        remote(skf.at[to], rkf.at[ctx], kf_s, kf_r, (to, ch)).start()
        return carry

    lax.fori_loop(1, 64, send_pair, 0)
    owe("kf_s", skf.at[pl.ds(0, 63)], kf_s)
    owe("kf_r", rkf.at[pl.ds(0, 63)], kf_r)
    for i in range(2):
        settle(f"far_r{i}")
        spread(gp, 1 - zh, 1, i)

    drain(wa.at[pl.ds(0, 2), 0], w_r.at[1])
    z24 = lax.rem(z2 + 4, 8)
    for block in (zl, z4, z2, z24):
        send_w(block, place(z1), 2).start()
    send_w(z2, sib, 3).start()
    send_w(z24, sib, 3).start()

    for i in range(2, 4):
        settle(f"far_r{i}")
        spread(gp, 1 - zh, 1, i)

    settle("grad_r0", "grad_r1")

    settle("p_r")
    first_core = core == 0

    def partial_rows(t, carry):
        left = ga[t // 4, pl.ds((t % 4) * 4, 4)].reshape(512, 128)
        part = lax.dot_general(
            left, pa[...].reshape(512, 512), (((0,), (0,)), ((), ())), preferred_element_type=F32
        )
        top, low = part[:64], part[64:]
        acc2[t] = jnp.where(first_core, top, low)
        sc[t] = jnp.where(first_core, low, top).astype(BF16)
        return carry

    lax.fori_loop(0, 8, partial_rows, 0)
    core_copy = remote(sc, rc, two_s.at[0], two_r.at[0], sib)
    core_copy.start()
    owed["core_s"], owed["core_r"] = core_copy.wait_send, core_copy.wait_recv

    drain(wa.at[pl.ds(0, 4), 0], w_r.at[2])
    for block in (z1, lax.rem(z1 + 4, 8), z1 + 2 - 4 * ((z1 // 2) % 2), lax.rem(z1 + 6 - 4 * ((z1 // 2) % 2), 8)):
        send_w(block, sib, 3).start()

    settle("core_r")
    bit0, bit1, bit2 = zl % 2, (zl // 2) % 2, zl // 4
    for i in range(4):
        give, keep = 2 * i + 1 - bit0, 2 * i + bit0
        sa[i] = (acc2[give] + rc[give].astype(F32)).astype(BF16)
        acc2[keep] = acc2[keep] + rc[keep].astype(F32)
    a_copy = remote(sa, ra, two_s.at[1], two_r.at[1], place(z1))
    a_copy.start()
    owed["a_s"], owed["a_r"] = a_copy.wait_send, a_copy.wait_recv

    settle("w_r3")

    acc1[...] = jnp.zeros_like(acc1)

    def multiply(row):
        def body(t, carry):
            left = ga[row, pl.ds(t * 4, 4)].reshape(512, 128)
            right = wa[row * 4 + t].reshape(128, 512)
            acc1[...] += jnp.dot(left, right, preferred_element_type=F32)
            return carry

        lax.fori_loop(0, 4, body, 0)

    multiply(zh)
    multiply(1 - zh)
    owe("one_s", s1, one_s)
    owe("one_r", r1, one_r)
    for d in range(1, 4):
        y_to = lax.rem(y + d, 4)
        s1[d - 1] = acc1[pl.ds(pl.multiple_of(y_to * 128, 128), 128), :].astype(BF16)
        remote(s1.at[d - 1], r1.at[d - 1], one_s, one_r, (zl * 8 + y_to * 2 + core, ch)).start()


    settle("a_r")
    for i in range(2):
        give, keep = 2 * i + 1 - bit1, 2 * i + bit1
        sb[i] = (acc2[2 * give + bit0] + ra[give].astype(F32)).astype(BF16)
        acc2[2 * keep + bit0] = acc2[2 * keep + bit0] + ra[keep].astype(F32)
    b_copy = remote(sb, rb, two_s.at[2], two_r.at[2], place(z2))
    b_copy.start()
    owed["b_s"], owed["b_r"] = b_copy.wait_send, b_copy.wait_recv

    settle("one_r")
    delta = acc1[pl.ds(pl.multiple_of(y * 128, 128), 128), :]
    for d in range(3):
        delta = delta + r1[d].astype(F32)
    conv = (delta * q_ref[...].astype(F32)).astype(BF16).astype(F32)
    sg[...] = conv.T.reshape(32, 16, 128).astype(BF16)
    rg[core, chip] = sg[chip]

    def send_conv(d, carry):
        to = lax.rem(chip + d, 32)
        remote(sg.at[to], rg.at[core, chip], g_s.at[0], g_r.at[0], (to * 2 + core, ch)).start()
        return carry

    lax.fori_loop(1, 32, send_conv, 0)
    qg_ref[...] = (delta * z_ref[...].astype(F32)).astype(BF16)
    owe("g_s", sg.at[pl.ds(0, 31)], g_s.at[0])
    owe("g_r", rg.at[0, pl.ds(0, 31)], g_r.at[0])

    settle("b_r")
    give, keep = 1 - bit2, bit2
    sd[...] = (acc2[4 * give + 2 * bit1 + bit0] + rb[give].astype(F32)).astype(BF16)
    d_copy = remote(sd, rd, two_s.at[3], two_r.at[3], place(z4))
    d_copy.start()
    owed["d_s"], owed["d_r"] = d_copy.wait_send, d_copy.wait_recv
    mine = acc2[4 * keep + 2 * bit1 + bit0] + rb[keep].astype(F32)
    wg_ref[...] = mine

    for copy in loads[7:]:
        copy.wait()
    twist_cos, twist_sin = twist_ref[0], twist_ref[1]

    def spectrum(base, table, slot):
        for c in range(8):
            dd[:, c * 128 : (c + 1) * 128] = fs[pl.ds(base + c, 64, stride=16), :].astype(BF16)
        both = jnp.dot(table[...], dd[...], preferred_element_type=F32)
        both = both[: 2 * HALF] + both[2 * HALF :]
        for c in range(8):
            real = both[:HALF, c * 128 : (c + 1) * 128]
            imag = both[HALF:, c * 128 : (c + 1) * 128]
            aa[c * HALF : (c + 1) * HALF, :128] = real * twist_cos + imag * twist_sin
            aa[c * HALF : (c + 1) * HALF, 128:] = imag * twist_cos - real * twist_sin
        spec[slot] = three(aa[...], forth_ref[0], forth_ref[1])

    settle("kf_r")
    fs[...] = rkf[...].astype(F32).reshape(1024, 128)
    spectrum(0, first_ref, 0)
    spectrum(8, first_ref, 1)

    settle("g_r")
    g_copy = remote(rg.at[core], rg.at[core], g_s.at[1], g_r.at[1], sib)
    g_copy.start()
    owed["gs_s"], owed["gs_r"] = g_copy.wait_send, g_copy.wait_recv

    settle("gs_r")
    fs[...] = rg[...].astype(F32).reshape(1024, 128)
    spectrum(core * 8, swapped_ref, 2)

    for slot, base in ((1, 0), (0, 8)):
        other_real, other_imag = spec[slot, :, :128], spec[slot, :, 128:]
        grad_real, grad_imag = spec[2, :, :128], spec[2, :, 128:]
        aa[:, :128] = other_real * grad_real + other_imag * grad_imag
        aa[:, 128:] = other_real * grad_imag - other_imag * grad_real
        turned = three(aa[...], back_ref[0], back_ref[1])
        for c in range(8):
            real = turned[c * HALF : (c + 1) * HALF, :128]
            imag = turned[c * HALF : (c + 1) * HALF, 128:]
            xx[:HALF, c * 128 : (c + 1) * 128] = real * twist_cos - imag * twist_sin
            xx[HALF:, c * 128 : (c + 1) * 128] = real * twist_sin + imag * twist_cos
        right = xx[...]
        right_high = right.astype(BF16)
        right_low = (right - right_high.astype(F32)).astype(BF16)
        signal = (
            jnp.dot(last_ref[0], right_high, preferred_element_type=F32)
            + jnp.dot(last_ref[0], right_low, preferred_element_type=F32)
            + jnp.dot(last_ref[1], right_high, preferred_element_type=F32)
        )
        for c in range(8):
            fs[pl.ds(base + c, 64, stride=16), :] = signal[:, c * 128 : (c + 1) * 128]
    sf[...] = fs[...].astype(BF16).reshape(64, 16, 128)
    rf[ctx] = sf[ctx]

    def send_back(d, carry):
        to = lax.rem(ctx + d, 64)
        remote(sf.at[to], rf.at[ctx], f_s, f_r, (to, ch)).start()
        return carry

    lax.fori_loop(1, 64, send_back, 0)
    owe("f_s", sf.at[pl.ds(0, 63)], f_s)
    owe("f_r", rf.at[pl.ds(0, 63)], f_r)

    settle("d_r")
    wg_ref[...] = wg_ref[...] + rd[...].astype(F32)

    settle("f_r")
    for t in range(4):
        back = rf[t * 16 : (t + 1) * 16].astype(F32)
        vd_ref[:, t * 128 : (t + 1) * 128] = back[:, :8].reshape(128, 128).T.astype(BF16)
        fg_ref[:, t * 128 : (t + 1) * 128] = back[:, 8:].reshape(128, 128).T.astype(BF16)
    settle()


def on_device(
    queries, keys, values, conv_out, filters, out_grad, out_weight, moment_one, moment_two
):
    tables = [jnp.asarray(t) for t in dft_tables()]
    vmem = pl.BlockSpec(memory_space=pltpu.VMEM)
    dma = pltpu.SemaphoreType.DMA

    def half(*shape):
        return pltpu.VMEM(shape, BF16)

    def full(*shape):
        return pltpu.VMEM(shape, F32)

    query_grad, value_delta, filter_grad, weight_grad = pl.pallas_call(
        kernel,
        out_shape=(
            jax.ShapeDtypeStruct((128, 512), BF16),
            jax.ShapeDtypeStruct((128, 512), BF16),
            jax.ShapeDtypeStruct((128, 512), BF16),
            jax.ShapeDtypeStruct((64, 512), F32),
        ),
        in_specs=[pl.BlockSpec(memory_space=pltpu.HBM)] * 13,
        out_specs=(vmem,) * 4,
        scratch_shapes=[
            *[half(128, 512)] * 6,
            *[pltpu.VMEM(t.shape, t.dtype) for t in tables],
            half(2, 16, 128, 128),
            half(128, 512),
            half(8, 2, 64, 512),
            half(4, 128, 512),
            half(64, 16, 128),
            half(64, 16, 128),
            half(3, 128, 512),
            half(3, 128, 512),
            full(512, 512),
            half(8, 64, 512),
            half(8, 64, 512),
            full(8, 64, 512),
            half(4, 64, 512),
            half(4, 64, 512),
            half(2, 64, 512),
            half(2, 64, 512),
            half(64, 512),
            half(64, 512),
            half(32, 16, 128),
            half(2, 32, 16, 128),
            half(64, 16, 128),
            half(64, 16, 128),
            full(1024, 128),
            half(64, 1024),
            full(8 * HALF, 256),
            full(3, 8 * HALF, 256),
            full(2 * HALF, 1024),
            dma((2,)), dma((2,)),
            dma((4,)), dma((4,)),
            dma((4,)), dma((4,)),
            dma, dma,
            dma, dma,
            dma, dma,
            dma((4,)), dma((4,)),
            dma((2,)), dma((2,)),
            dma, dma,
            dma((13,)),
        ],
        compiler_params=pltpu.CompilerParams(
            collective_id=1, has_side_effects=True, vmem_limit_bytes=60 * 2**20
        ),
    )(queries, keys, values, conv_out, filters, out_grad, out_weight, *tables)

    delta = value_delta.astype(F32)
    key_grad = (delta * values.astype(F32)).astype(BF16)
    value_grad = (delta * keys.astype(F32)).astype(BF16)
    new_moment_one = BETA_ONE * moment_one + (1.0 - BETA_ONE) * weight_grad
    new_moment_two = BETA_TWO * moment_two + (1.0 - BETA_TWO) * weight_grad * weight_grad
    corr_one = 1.0 - BETA_ONE**10
    corr_two = 1.0 - BETA_TWO**10
    weight_float = out_weight.astype(F32)
    update = new_moment_one / corr_one / (jnp.sqrt(new_moment_two / corr_two) + ADAM_STABILIZER)
    new_weight = (weight_float - STEP_RATE * (update + DECAY * weight_float)).astype(BF16)
    return (
        query_grad,
        key_grad,
        value_grad,
        filter_grad,
        new_weight,
        new_moment_one,
        new_moment_two,
    )


def solution(mesh):
    spec = P("ctx", "ch")
    return jax.shard_map(
        on_device, mesh=mesh, in_specs=(spec,) * 9, out_specs=(spec,) * 7, check_vma=False
    )
```
